32 devices in a mesh: parts: 2 (over y), row: 4 (over z), dim: 4 (over x, core).
Axes of the slice: x: 2, y: 2, z: 4, core: 2. Of those that a mesh axis runs over, the one named last changes fastest.
Arguments:
- train_grads: bfloat16 [8192, 8192], P(('parts', 'row'), 'dim'), parts along dimension 0, may hold values from -16 to 16
- precond: float32 [8192], P('dim'), may hold values from 0.25 to 20
- query_store: bfloat16 [8, 256, 8192], P(('parts', 'row'), None, 'dim'), parts along dimension 0, may hold values from -16 to 16
- owner: int32 [8], P('parts'), parts along dimension 0, may hold values from 0 to 3, as said below
- order: int32 [8], P('parts'), parts along dimension 0, may hold values from 0 to 3, each once
Outputs:
- scores: float32 [4, 8192, 256], P(None, ('parts', 'row', 'dim')), parts along dimension 1
The draws below stay inside these ranges and needn't reach their ends.
There are 2 independent parts, one for each index of `parts`. The reference program is written for one: setup_inputs(seed, part) draws one part's arguments, and reference() takes and returns one part's arrays. A program takes and returns all parts, laid end to end along the dimension named above; an argument that names none is the same for every part. Nothing has to cross between parts.
Inputs may be any that keep to these rules, and one draw needn't show every extreme that they name: `owner`: distinct slots; slot 0 and slot 3 each hold one of the blocks.
All inputs are finite; a program needn't handle non-finite values.
Results may differ from the reference program's by a relative error of at most 0.008.
Values may be sent and summed in bfloat16 or wider, within the bound.
A program may use at most 64 MiB of HBM per device.

```python
import jax
import jax.numpy as jnp
from jax import lax

K = 8192
QB = 256
NB = 4
TR = 1024
TRAIN = 4096
SLOTS = 4
N_ROW = 4
N_DIM = 4


def gradient_rows(key, count):
    key_rows, key_vals = jax.random.split(key, 2)
    scales = jnp.exp(jax.random.uniform(key_rows, (count, 1), jnp.float32, 0.0, jnp.log(10.0))) / 3.0
    values = jnp.clip(jax.random.normal(key_vals, (count, K), jnp.float32), -4.0, 4.0)
    return scales * values


def draw_train_grads(key, part):
    key = jax.random.fold_in(key, 11)
    return gradient_rows(key, TRAIN).astype(jnp.bfloat16)


def draw_query_store(key, part):
    key = jax.random.fold_in(key, 23)
    return gradient_rows(key, SLOTS * QB).reshape(SLOTS, QB, K).astype(jnp.bfloat16)


def draw_precond(key, part):
    key = jax.random.fold_in(key, 37)
    place = jnp.arange(K, dtype=jnp.float32) / (K - 1)
    rough = jnp.exp(jax.random.uniform(key, (K,), jnp.float32, jnp.log(0.5), jnp.log(2.0)))
    return jnp.exp(jnp.log(3.0) * place) * rough


def draw_owner(key, part):
    key = jax.random.fold_in(key, 41)
    key_pick, key_place = jax.random.split(key)
    middle = jax.random.permutation(key_pick, SLOTS - 2).astype(jnp.int32) + 1
    picks = jnp.concatenate([jnp.array([0, SLOTS - 1], jnp.int32), middle[:NB - 2]])
    places = jax.random.permutation(key_place, NB)
    return picks[places].astype(jnp.int32)


def setup_inputs(seed: int = 0, part: int = 0) -> dict:
    splits = jax.random.split(jax.random.key(seed), 6)
    part_splits = jax.random.split(jax.random.fold_in(splits[5], part), 6)
    return {
        "train_grads": draw_train_grads(jax.random.fold_in(jax.random.fold_in(splits[5], part), 71), part),
        "precond": draw_precond(jax.random.fold_in(splits[5], 71), part),
        "query_store": draw_query_store(jax.random.fold_in(jax.random.fold_in(splits[5], part), 71), part),
        "owner": draw_owner(jax.random.fold_in(jax.random.fold_in(splits[5], part), 71), part),
        "order": jax.random.permutation(part_splits[4], NB).astype(jnp.int32),
    }


def row_norms(train_grads, precond):
    blocks = train_grads.reshape(N_ROW, TR, K)

    def one(block):
        wide = block.astype(jnp.float32)
        return lax.optimization_barrier(jnp.sum(wide * wide * precond[None, :], axis=1)) / K
    return lax.map(one, blocks).reshape(TRAIN)

def grouped_product(train_grads, weighted):
    width = K // N_DIM
    left = train_grads.reshape(TRAIN, N_DIM, width).transpose(1, 0, 2)
    right = weighted.reshape(QB, N_DIM, width).transpose(1, 0, 2)

    def add_group(total, pieces):
        part = lax.dot_general(pieces[0], pieces[1], (((1,), (1,)), ((), ())), preferred_element_type=jnp.float32)
        return (total + part.astype(jnp.bfloat16).astype(jnp.float32), None)
    total, _ = lax.scan(add_group, jnp.zeros((TRAIN, QB), jnp.float32), (left, right))
    return total

def reference(train_grads, precond, query_store, owner, order):
    gsq = row_norms(train_grads, precond)
    tiles = []
    for step in range(NB):
        block = query_store[owner[order[step]]]
        wide = block.astype(jnp.float32)
        qsq = lax.optimization_barrier(jnp.sum(wide * wide * precond[None, :], axis=1)) / K
        weighted = (wide * precond[None, :]).astype(jnp.bfloat16)
        raw = grouped_product(train_grads, weighted)
        tiles.append(raw / jnp.sqrt(K * (gsq[:, None] + 1e-06) * (qsq[None, :] + 1e-06)))
    return jnp.stack(tiles)
```

```python
import functools

import jax
import jax.numpy as jnp
from jax import lax
from jax.experimental import pallas as pl
from jax.experimental.pallas import tpu as pltpu
from jax.sharding import PartitionSpec as P

K = 8192
NB = 4
CHUNK = 64
AHEAD = 2
MESH = pl.DeviceIdType.MESH
NT = (((1,), (1,)), ((), ()))


def row_sums(values, precond):
    wide = values.astype(jnp.float32)
    squares = wide * wide * precond
    lanes = squares[:, :128]
    for at in range(128, squares.shape[1], 128):
        lanes = lanes + squares[:, at : at + 128]
    return jnp.sum(lanes.T, axis=0, keepdims=True)


def score_kernel(
    n_row, n_dim, train_hbm, precond_ref, slot_hbm, raw_ref, g_ref, q_ref,
    train, slot, blocks, parts, landed, g_out, g_in, q_out, q_in, q_sum, q_all,
    load_sem, hop_send, hop_recv, part_send, part_recv, norm_send, norm_recv, q_send, q_recv,
):
    z = lax.axis_index("row")
    d = lax.axis_index("dim")
    rows = train.shape[0]
    queries = slot.shape[0]
    share = rows // n_dim
    steps = queries // CHUNK
    half = 2 * CHUNK

    load_slot = pltpu.make_async_copy(slot_hbm, slot, load_sem.at[0])
    load_train = pltpu.make_async_copy(train_hbm, train, load_sem.at[1])
    load_slot.start()
    load_train.start()

    barrier = pltpu.get_barrier_semaphore()
    for r in range(1, n_row):
        pl.semaphore_signal(barrier, inc=1, device_id={"row": lax.rem(z + r, n_row)}, device_id_type=MESH)
    for r in range(1, n_dim):
        pl.semaphore_signal(barrier, inc=1, device_id={"dim": lax.rem(d + r, n_dim)}, device_id_type=MESH)

    def rows_of(c):
        return pl.ds(pl.multiple_of(c * CHUNK, CHUNK), CHUNK)

    def hop(way, b, c):
        to = z + 1 if way == 0 else z - 1
        piece = blocks.at[b, rows_of(c)]
        return pltpu.make_async_remote_copy(
            src_ref=piece, dst_ref=piece, send_sem=hop_send.at[way, b, c], recv_sem=hop_recv.at[b, c],
            device_id={"row": to}, device_id_type=MESH,
        )

    def send_part(b, c, r):
        to = lax.rem(d + r, n_dim)
        return pltpu.make_async_remote_copy(
            src_ref=parts.at[b, to, rows_of(c)], dst_ref=landed.at[b, d, rows_of(c)],
            send_sem=part_send.at[b, r, c], recv_sem=part_recv.at[b, r, c],
            device_id={"dim": to}, device_id_type=MESH,
        )

    def weigh(c):
        blocks[z, rows_of(c), :] = (slot[rows_of(c), :].astype(jnp.float32) * precond_ref[...]).astype(jnp.bfloat16)

    def send_own(c):
        pl.when(z < n_row - 1)(lambda: hop(0, z, c).start())
        pl.when(z > 0)(lambda: hop(1, z, c).start())

    def product(b, c):
        weighted = blocks[b, rows_of(c), :]
        for r in PART_ORDER(n_dim):
            to = lax.rem(d + r, n_dim)
            mine = train[pl.ds(pl.multiple_of(to * share, share), share), :]
            part = lax.dot_general(weighted, mine, NT, preferred_element_type=jnp.float32)
            parts[b, to, rows_of(c), :] = part.astype(jnp.bfloat16)
            if r:
                send_part(b, c, r).start()

    def add_up(b, which):
        for k in range(2):
            for r in range(1, n_dim):
                send_part(b, which * 2 + k, r).wait_recv()
        at = pl.ds(which * half, half)
        total = parts[b, d, at, :].astype(jnp.float32)
        for r in range(1, n_dim):
            total = total + landed[b, lax.rem(d + r, n_dim), at, :].astype(jnp.float32)
        raw_ref[b, :, at] = total.T

    def each_block(h, run):
        if h == 0:
            run(z)
        elif h < n_row:
            pl.when(z - h >= 0)(lambda: run(z - h))
            pl.when(z + h < n_row)(lambda: run(z + h))

    load_slot.wait()
    for c in range(AHEAD):
        weigh(c)
    pl.semaphore_wait(barrier, n_row - 1 + n_dim - 1)
    for c in range(AHEAD):
        send_own(c)
    for c in range(AHEAD, steps):
        weigh(c)

    q_out[...] = jnp.broadcast_to(row_sums(slot[...], precond_ref[...]), q_out.shape)

    def norm_copy(r, which):
        to = lax.rem(d + r, n_dim)
        src, dst = (g_out.at[to], g_in.at[d]) if which == 0 else (q_out, q_in.at[d])
        return pltpu.make_async_remote_copy(
            src_ref=src, dst_ref=dst, send_sem=norm_send.at[which, r], recv_sem=norm_recv.at[which, r],
            device_id={"dim": to}, device_id_type=MESH,
        )

    def q_copy(r):
        return pltpu.make_async_remote_copy(
            src_ref=q_sum, dst_ref=q_all.at[z], send_sem=q_send.at[r], recv_sem=q_recv.at[r],
            device_id={"row": lax.rem(z + r, n_row)}, device_id_type=MESH,
        )

    for r in range(1, n_dim):
        norm_copy(r, 1).start()
    load_train.wait()

    def train_norms(t):
        at = pl.ds(pl.multiple_of(t * share, share), share)
        g_out[t] = jnp.broadcast_to(row_sums(train[at, :], precond_ref[...]), g_out.shape[1:])

    for h in range(1, n_row):

        def step(c, carry, h=h):
            def arrive_left():
                hop(0, z - h, c).wait_recv()
                pl.when(z < n_row - 1)(lambda: hop(0, z - h, c).start())

            def arrive_right():
                hop(1, z + h, c).wait_recv()
                pl.when(z > 0)(lambda: hop(1, z + h, c).start())

            if h == 1:
                product(z, c)
            pl.when(z - h >= 0)(arrive_left)
            pl.when(z + h < n_row)(arrive_right)
            if h == 1:
                pl.when(c + AHEAD < steps)(lambda: send_own(c + AHEAD))
            each_block(h, lambda b: product(b, c))
            for which in range(steps // 2):
                if which == 0:
                    pl.when(c == 0)(lambda: each_block(h - 1, lambda b: add_up(b, steps // 2 - 1)) if h > 1 else None)
                else:
                    pl.when(c == 2 * which)(lambda which=which: each_block(h, lambda b: add_up(b, which - 1)))
            if h == 1:
                pl.when(c < n_dim)(lambda: train_norms(c))
            return carry

        lax.fori_loop(0, steps, step, 0)
        if h == 1:
            for t in range(steps, n_dim):
                train_norms(t)
            for r in range(1, n_dim):
                norm_copy(r, 0).start()
            for r in range(1, n_dim):
                norm_copy(r, 1).wait_recv()
            total = q_out[...]
            for r in range(1, n_dim):
                total = total + q_in[lax.rem(d + r, n_dim)]
            q_sum[...] = total
            q_ref[z] = total
            for r in range(1, n_row):
                q_copy(r).start()
            for which in range(steps // 2):
                add_up(z, which)
            for r in range(1, n_dim):
                norm_copy(r, 0).wait_recv()
            total = g_out[d]
            for r in range(1, n_dim):
                total = total + g_in[lax.rem(d + r, n_dim)]
            g_ref[...] = total
        if h == 2:
            for r in range(1, n_row):
                q_copy(r).wait_recv()
            for r in range(1, n_row):
                other = lax.rem(z + r, n_row)
                q_ref[other] = q_all[other]
    each_block(n_row - 1, lambda b: add_up(b, steps // 2 - 1))

    def sent(c, carry):
        for b in range(n_row):
            pl.when((z < n_row - 1) & (b <= z))(lambda b=b: hop(0, b, c).wait_send())
            pl.when((z > 0) & (b >= z))(lambda b=b: hop(1, b, c).wait_send())
            for r in range(1, n_dim):
                send_part(b, c, r).wait_send()
        return carry

    lax.fori_loop(0, steps, sent, 0)
    for r in range(1, n_dim):
        norm_copy(r, 0).wait_send()
        norm_copy(r, 1).wait_send()
    for r in range(1, n_row):
        q_copy(r).wait_send()


def PART_ORDER(n_dim):
    middle = n_dim // 2
    return [middle] + [r for r in range(1, n_dim) if r != middle] + [0]


def raw_scores(n_row, n_dim, train_grads, precond, slot):
    rows, width = train_grads.shape
    queries = slot.shape[0]
    share = rows // n_dim
    steps = queries // CHUNK
    f32, bf16 = jnp.float32, jnp.bfloat16
    vmem = pl.BlockSpec(memory_space=pltpu.VMEM)
    anywhere = pl.BlockSpec(memory_space=pl.ANY)
    dma = pltpu.SemaphoreType.DMA
    return pl.pallas_call(
        functools.partial(score_kernel, n_row, n_dim),
        out_shape=(
            jax.ShapeDtypeStruct((n_row, share, queries), f32),
            jax.ShapeDtypeStruct((8, share), f32),
            jax.ShapeDtypeStruct((n_row, 8, queries), f32),
        ),
        in_specs=[anywhere, vmem, anywhere],
        out_specs=(vmem, vmem, vmem),
        scratch_shapes=[
            pltpu.VMEM((rows, width), bf16),
            pltpu.VMEM((queries, width), bf16),
            pltpu.VMEM((n_row, queries, width), bf16),
            pltpu.VMEM((n_row, n_dim, queries, share), bf16),
            pltpu.VMEM((n_row, n_dim, queries, share), bf16),
            pltpu.VMEM((n_dim, 8, share), f32),
            pltpu.VMEM((n_dim, 8, share), f32),
            pltpu.VMEM((8, queries), f32),
            pltpu.VMEM((n_dim, 8, queries), f32),
            pltpu.VMEM((8, queries), f32),
            pltpu.VMEM((n_row, 8, queries), f32),
            dma((2,)),
            dma((2, n_row, steps)),
            dma((n_row, steps)),
            dma((n_row, n_dim, steps)),
            dma((n_row, n_dim, steps)),
            dma((2, n_dim)),
            dma((2, n_dim)),
            dma((n_row,)),
            dma((n_row,)),
        ],
        compiler_params=pltpu.CompilerParams(
            collective_id=0, has_side_effects=True, vmem_limit_bytes=48 * 1024 * 1024
        ),
        name="scores_raw",
    )(train_grads, precond.reshape(1, width), slot)


def normalise_kernel(owner, order, raw_ref, g_ref, q_ref, out_ref):
    queries = raw_ref.shape[2]
    share = raw_ref.shape[1]
    g = lax.rsqrt(K * (g_ref[0:1, :] / K + 1e-06))
    column = jnp.broadcast_to(g, (128, share)).T
    q = lax.rsqrt(q_ref[0, 0:1, :] / K + 1e-06)
    for at in range(0, queries, 128):
        out_ref[0, :, at : at + 128] = raw_ref[0, :, at : at + 128] * column * q[:, at : at + 128]


def normalise(raw, g, q, owner, order):
    n, share, queries = raw.shape
    return pl.pallas_call(
        normalise_kernel,
        out_shape=jax.ShapeDtypeStruct((NB, share, queries), jnp.float32),
        grid_spec=pltpu.PrefetchScalarGridSpec(
            num_scalar_prefetch=2,
            grid=(NB,),
            in_specs=[
                pl.BlockSpec((1, share, queries), lambda s, owner, order: (owner[order[s]], 0, 0)),
                pl.BlockSpec((8, share), lambda s, owner, order: (0, 0)),
                pl.BlockSpec((1, 8, queries), lambda s, owner, order: (owner[order[s]], 0, 0)),
            ],
            out_specs=pl.BlockSpec((1, share, queries), lambda s, owner, order: (s, 0, 0)),
        ),
        name="normalise",
    )(owner, order, raw, g, q)


def every_slot(train_grads, precond, query_store, owner, order):
    raw, g, q = raw_scores(lax.axis_size("row"), lax.axis_size("dim"), train_grads, precond, query_store[0])
    return normalise(raw, g, q, owner, order)


def weighted_norm(values, precond):
    wide = values.astype(jnp.float32)
    return jnp.sum(wide * wide * precond[None, :], axis=1) / K


def some_slots(train_grads, precond, query_store, owner, order):
    share = train_grads.shape[0] // lax.axis_size("dim")
    slot = query_store[0]
    roots = owner[order]
    mine = (roots == lax.axis_index("row"))[:, None, None]
    blocks = lax.psum(jnp.where(mine, slot[None], 0).astype(jnp.bfloat16), "row")
    gsq = lax.psum_scatter(weighted_norm(train_grads, precond), "dim", tiled=True)
    results = []
    for step in range(NB):
        block = blocks[step]
        qsq = lax.psum(weighted_norm(block, precond), "dim")
        weighted = (block.astype(jnp.float32) * precond[None, :]).astype(jnp.bfloat16)
        part = lax.dot_general(train_grads, weighted, NT, preferred_element_type=jnp.float32)
        summed = lax.psum_scatter(part.astype(jnp.bfloat16), "dim", scatter_dimension=0, tiled=True)
        scale = jnp.sqrt(K * (gsq[:, None] + 1e-06) * (qsq[None, :] + 1e-06))
        results.append(summed.astype(jnp.float32) / scale)
    return jnp.stack(results)


def solution(mesh):
    return jax.shard_map(
        every_slot if mesh.shape["row"] == NB else some_slots,
        mesh=mesh,
        in_specs=(
            P(("parts", "row"), "dim"),
            P("dim"),
            P(("parts", "row"), None, "dim"),
            P("parts"),
            P("parts"),
        ),
        out_specs=P(None, ("parts", "row", "dim"), None),
        check_vma=False,
    )
```

```python
import functools

import jax
import jax.numpy as jnp
from jax import lax
from jax.experimental import pallas as pl
from jax.experimental.pallas import tpu as pltpu
from jax.sharding import PartitionSpec as P

K = 8192
NB = 4
CHUNK = 128
AHEAD = 2
MESH = pl.DeviceIdType.MESH
NT = (((1,), (1,)), ((), ()))


def row_sums(values, precond):
    wide = values.astype(jnp.float32)
    squares = wide * wide * precond
    lanes = squares[:, :128]
    for at in range(128, squares.shape[1], 128):
        lanes = lanes + squares[:, at : at + 128]
    return jnp.sum(lanes.T, axis=0, keepdims=True)


def score_kernel(
    n_row, n_dim, owner_ref, order_ref, train_hbm, precond_hbm, slot_hbm, out_ref,
    raw_ref, column, q_ref, train, precond_ref, slot, blocks, parts, landed, g_out, g_in, q_out, q_in, q_sum, q_all,
    load_sem, hop_send, hop_recv, part_send, part_recv, norm_send, norm_recv, q_send, q_recv,
):
    z = lax.axis_index("row")
    d = lax.axis_index("dim")
    rows = train.shape[0]
    queries = slot.shape[0]
    share = rows // n_dim
    steps = queries // CHUNK

    load_slot = pltpu.make_async_copy(slot_hbm, slot, load_sem.at[0])
    load_train = pltpu.make_async_copy(train_hbm, train, load_sem.at[1])
    load_precond = pltpu.make_async_copy(precond_hbm, precond_ref, load_sem.at[2])
    load_precond.start()
    load_slot.start()
    load_train.start()

    barrier = pltpu.get_barrier_semaphore()
    for r in range(1, n_row):
        pl.semaphore_signal(barrier, inc=1, device_id={"row": lax.rem(z + r, n_row)}, device_id_type=MESH)
    for r in range(1, n_dim):
        pl.semaphore_signal(barrier, inc=1, device_id={"dim": lax.rem(d + r, n_dim)}, device_id_type=MESH)

    def rows_of(c):
        return pl.ds(pl.multiple_of(c * CHUNK, CHUNK), CHUNK)

    def hop(way, b, c):
        to = z + 1 if way == 0 else z - 1
        piece = blocks.at[b, rows_of(c)]
        return pltpu.make_async_remote_copy(
            src_ref=piece, dst_ref=piece, send_sem=hop_send.at[way, b, c], recv_sem=hop_recv.at[b, c],
            device_id={"row": to}, device_id_type=MESH,
        )

    def send_part(b, c, r):
        to = lax.rem(d + r, n_dim)
        return pltpu.make_async_remote_copy(
            src_ref=parts.at[b, c, to], dst_ref=landed.at[b, c, d],
            send_sem=part_send.at[b, r, c], recv_sem=part_recv.at[b, r, c],
            device_id={"dim": to}, device_id_type=MESH,
        )

    def weigh(c):
        blocks[z, rows_of(c), :] = (slot[rows_of(c), :].astype(jnp.float32) * precond_ref[...]).astype(jnp.bfloat16)

    def send_own(c):
        pl.when(z < n_row - 1)(lambda: hop(0, z, c).start())
        pl.when(z > 0)(lambda: hop(1, z, c).start())

    def product(b, c):
        weighted = blocks[b, rows_of(c), :]
        for r in PART_ORDER(n_dim):
            to = lax.rem(d + r, n_dim)
            mine = train[pl.ds(pl.multiple_of(to * share, share), share), :]
            part = lax.dot_general(mine, weighted, NT, preferred_element_type=jnp.float32)
            parts[b, c, to] = part.astype(jnp.bfloat16)
            if r:
                send_part(b, c, r).start()

    def add_up(b, c):
        for r in range(1, n_dim):
            send_part(b, c, r).wait_recv()
        total = parts[b, c, d].astype(jnp.float32)
        for r in range(1, n_dim):
            total = total + landed[b, c, lax.rem(d + r, n_dim)].astype(jnp.float32)
        raw_ref[b, c] = total

    def each_block(h, run):
        if h == 0:
            run(z)
        elif h < n_row:
            pl.when(z - h >= 0)(lambda: run(z - h))
            pl.when(z + h < n_row)(lambda: run(z + h))

    load_precond.wait()
    load_slot.wait()
    for c in range(AHEAD):
        weigh(c)
    pl.semaphore_wait(barrier, n_row - 1 + n_dim - 1)
    for c in range(AHEAD):
        send_own(c)
    for c in range(AHEAD, steps):
        weigh(c)

    q_out[...] = jnp.broadcast_to(row_sums(slot[...], precond_ref[...]), q_out.shape)

    def norm_copy(r, which):
        to = lax.rem(d + r, n_dim)
        src, dst = (g_out.at[to], g_in.at[d]) if which == 0 else (q_out, q_in.at[d])
        return pltpu.make_async_remote_copy(
            src_ref=src, dst_ref=dst, send_sem=norm_send.at[which, r], recv_sem=norm_recv.at[which, r],
            device_id={"dim": to}, device_id_type=MESH,
        )

    def q_copy(r):
        return pltpu.make_async_remote_copy(
            src_ref=q_sum, dst_ref=q_all.at[z], send_sem=q_send.at[r], recv_sem=q_recv.at[r],
            device_id={"row": lax.rem(z + r, n_row)}, device_id_type=MESH,
        )

    for r in range(1, n_dim):
        norm_copy(r, 1).start()
    load_train.wait()

    def train_norms(t):
        at = pl.ds(pl.multiple_of(t * share, share), share)
        g_out[t] = jnp.broadcast_to(row_sums(train[at, :], precond_ref[...]), g_out.shape[1:])

    for h in range(1, n_row):

        def step(c, carry, h=h):
            def arrive_left():
                hop(0, z - h, c).wait_recv()
                pl.when(z < n_row - 1)(lambda: hop(0, z - h, c).start())

            def arrive_right():
                hop(1, z + h, c).wait_recv()
                pl.when(z > 0)(lambda: hop(1, z + h, c).start())

            if h == 1:
                product(z, c)
            pl.when(z - h >= 0)(arrive_left)
            pl.when(z + h < n_row)(arrive_right)
            if h == 1:
                pl.when(c + AHEAD < steps)(lambda: send_own(c + AHEAD))
            each_block(h, lambda b: product(b, c))
            if h > 1:
                pl.when(c == 0)(lambda: each_block(h - 1, lambda b: add_up(b, steps - 1)))
            pl.when(c > 0)(lambda: each_block(h, lambda b: add_up(b, c - 1)))
            if h == 1:
                pl.when(c < n_dim)(lambda: train_norms(c))
            return carry

        lax.fori_loop(0, steps, step, 0)
        if h == 1:
            for t in range(steps, n_dim):
                train_norms(t)
            for r in range(1, n_dim):
                norm_copy(r, 0).start()
            for r in range(1, n_dim):
                norm_copy(r, 1).wait_recv()
            total = q_out[...]
            for r in range(1, n_dim):
                total = total + q_in[lax.rem(d + r, n_dim)]
            q_sum[...] = total
            q_ref[z] = lax.rsqrt(total / K + 1e-06)
            for r in range(1, n_row):
                q_copy(r).start()
            for c in range(steps):
                add_up(z, c)
            for r in range(1, n_dim):
                norm_copy(r, 0).wait_recv()
            total = g_out[d]
            for r in range(1, n_dim):
                total = total + g_in[lax.rem(d + r, n_dim)]
            g = lax.rsqrt(K * (total[0:1, :] / K + 1e-06))
            column[...] = jnp.broadcast_to(g, (128, share)).T
        if h == 2:
            for r in range(1, n_row):
                q_copy(r).wait_recv()
            for r in range(1, n_row):
                other = lax.rem(z + r, n_row)
                q_ref[other] = lax.rsqrt(q_all[other] / K + 1e-06)
    each_block(n_row - 1, lambda b: add_up(b, steps - 1))
    for s in range(NB):
        root = owner_ref[order_ref[s]]
        q = q_ref[root]
        for c in range(steps):
            at = slice(c * CHUNK, (c + 1) * CHUNK)
            out_ref[s, :, at] = raw_ref[root, c] * column[...] * q[0:1, at]

    def sent(c, carry):
        for b in range(n_row):
            pl.when((z < n_row - 1) & (b <= z))(lambda b=b: hop(0, b, c).wait_send())
            pl.when((z > 0) & (b >= z))(lambda b=b: hop(1, b, c).wait_send())
            for r in range(1, n_dim):
                send_part(b, c, r).wait_send()
        return carry

    lax.fori_loop(0, steps, sent, 0)
    for r in range(1, n_dim):
        norm_copy(r, 0).wait_send()
        norm_copy(r, 1).wait_send()
    for r in range(1, n_row):
        q_copy(r).wait_send()


def PART_ORDER(n_dim):
    middle = n_dim // 2
    return [middle] + [r for r in range(1, n_dim) if r != middle] + [0]


def scores(n_row, n_dim, owner, order, train_grads, precond, slot):
    rows, width = train_grads.shape
    queries = slot.shape[0]
    share = rows // n_dim
    steps = queries // CHUNK
    f32, bf16 = jnp.float32, jnp.bfloat16
    vmem = pl.BlockSpec(memory_space=pltpu.VMEM)
    hbm = pl.BlockSpec(memory_space=pltpu.HBM)
    smem = pl.BlockSpec(memory_space=pltpu.SMEM)
    dma = pltpu.SemaphoreType.DMA
    return pl.pallas_call(
        functools.partial(score_kernel, n_row, n_dim),
        out_shape=jax.ShapeDtypeStruct((NB, share, queries), f32),
        in_specs=[smem, smem, hbm, hbm, hbm],
        out_specs=vmem,
        scratch_shapes=[
            pltpu.VMEM((n_row, steps, share, CHUNK), f32),
            pltpu.VMEM((share, 128), f32),
            pltpu.VMEM((n_row, 8, queries), f32),
            pltpu.VMEM((rows, width), bf16),
            pltpu.VMEM((1, width), f32),
            pltpu.VMEM((queries, width), bf16),
            pltpu.VMEM((n_row, queries, width), bf16),
            pltpu.VMEM((n_row, steps, n_dim, share, CHUNK), bf16),
            pltpu.VMEM((n_row, steps, n_dim, share, CHUNK), bf16),
            pltpu.VMEM((n_dim, 8, share), f32),
            pltpu.VMEM((n_dim, 8, share), f32),
            pltpu.VMEM((8, queries), f32),
            pltpu.VMEM((n_dim, 8, queries), f32),
            pltpu.VMEM((8, queries), f32),
            pltpu.VMEM((n_row, 8, queries), f32),
            dma((3,)),
            dma((2, n_row, steps)),
            dma((n_row, steps)),
            dma((n_row, n_dim, steps)),
            dma((n_row, n_dim, steps)),
            dma((2, n_dim)),
            dma((2, n_dim)),
            dma((n_row,)),
            dma((n_row,)),
        ],
        compiler_params=pltpu.CompilerParams(
            collective_id=0, has_side_effects=True, vmem_limit_bytes=48 * 1024 * 1024
        ),
        name="scores",
    )(owner, order, train_grads, precond.reshape(1, width), slot)


def every_slot(train_grads, precond, query_store, owner, order):
    return scores(lax.axis_size("row"), lax.axis_size("dim"), owner, order, train_grads, precond, query_store[0])


def weighted_norm(values, precond):
    wide = values.astype(jnp.float32)
    return jnp.sum(wide * wide * precond[None, :], axis=1) / K


def some_slots(train_grads, precond, query_store, owner, order):
    share = train_grads.shape[0] // lax.axis_size("dim")
    slot = query_store[0]
    roots = owner[order]
    mine = (roots == lax.axis_index("row"))[:, None, None]
    blocks = lax.psum(jnp.where(mine, slot[None], 0).astype(jnp.bfloat16), "row")
    gsq = lax.psum_scatter(weighted_norm(train_grads, precond), "dim", tiled=True)
    results = []
    for step in range(NB):
        block = blocks[step]
        qsq = lax.psum(weighted_norm(block, precond), "dim")
        weighted = (block.astype(jnp.float32) * precond[None, :]).astype(jnp.bfloat16)
        part = lax.dot_general(train_grads, weighted, NT, preferred_element_type=jnp.float32)
        summed = lax.psum_scatter(part.astype(jnp.bfloat16), "dim", scatter_dimension=0, tiled=True)
        scale = jnp.sqrt(K * (gsq[:, None] + 1e-06) * (qsq[None, :] + 1e-06))
        results.append(summed.astype(jnp.float32) / scale)
    return jnp.stack(results)


def solution(mesh):
    return jax.shard_map(
        every_slot if mesh.shape["row"] == NB else some_slots,
        mesh=mesh,
        in_specs=(
            P(("parts", "row"), "dim"),
            P("dim"),
            P(("parts", "row"), None, "dim"),
            P("parts"),
            P("parts"),
        ),
        out_specs=P(None, ("parts", "row", "dim"), None),
        check_vma=False,
    )
```

```python
import functools

import jax
import jax.numpy as jnp
from jax import lax
from jax.experimental import pallas as pl
from jax.experimental.pallas import tpu as pltpu
from jax.sharding import PartitionSpec as P

K = 8192
NB = 4
CHUNK = 128
AHEAD = 2
VMEM_MIB = 63
MESH = pl.DeviceIdType.MESH
NT = (((1,), (1,)), ((), ()))


def row_sums(values, precond):
    wide = values.astype(jnp.float32)
    squares = wide * wide * precond
    lanes = squares[:, :128]
    for at in range(128, squares.shape[1], 128):
        lanes = lanes + squares[:, at : at + 128]
    return jnp.sum(lanes.T, axis=0, keepdims=True)


def score_kernel(
    n_row, n_dim, owner_hbm, order_hbm, train_hbm, precond_hbm, slot_hbm, out_ref,
    owner_ref, order_ref, raw_ref, column, q_ref, train, precond_ref, slot, blocks, parts, landed, g_out, g_in, q_out, q_in, q_sum, q_all,
    load_sem, hop_send, hop_recv, part_send, part_recv, norm_send, norm_recv, q_send, q_recv,
):
    z = lax.axis_index("row")
    d = lax.axis_index("dim")
    rows = train.shape[0]
    queries = slot.shape[0]
    share = rows // n_dim
    steps = queries // CHUNK

    load_slot = pltpu.make_async_copy(slot_hbm, slot, load_sem.at[0])
    load_train = pltpu.make_async_copy(train_hbm, train, load_sem.at[1])
    load_precond = pltpu.make_async_copy(precond_hbm, precond_ref, load_sem.at[2])
    load_owner = pltpu.make_async_copy(owner_hbm, owner_ref, load_sem.at[3])
    load_order = pltpu.make_async_copy(order_hbm, order_ref, load_sem.at[4])
    load_precond.start()
    load_slot.start()
    load_train.start()
    load_owner.start()
    load_order.start()

    barrier = pltpu.get_barrier_semaphore()
    for r in range(1, n_row):
        pl.semaphore_signal(barrier, inc=1, device_id={"row": lax.rem(z + r, n_row)}, device_id_type=MESH)
    for r in range(1, n_dim):
        pl.semaphore_signal(barrier, inc=1, device_id={"dim": lax.rem(d + r, n_dim)}, device_id_type=MESH)

    def rows_of(c):
        return pl.ds(pl.multiple_of(c * CHUNK, CHUNK), CHUNK)

    def hop(way, b, c):
        to = z + 1 if way == 0 else z - 1
        piece = blocks.at[b, rows_of(c)]
        return pltpu.make_async_remote_copy(
            src_ref=piece, dst_ref=piece, send_sem=hop_send.at[way, b, c], recv_sem=hop_recv.at[b, c],
            device_id={"row": to}, device_id_type=MESH,
        )

    def send_part(b, c, r):
        to = lax.rem(d + r, n_dim)
        return pltpu.make_async_remote_copy(
            src_ref=parts.at[b, c, to], dst_ref=landed.at[b, c, d],
            send_sem=part_send.at[b, r, c], recv_sem=part_recv.at[b, r, c],
            device_id={"dim": to}, device_id_type=MESH,
        )

    def weigh(c):
        blocks[z, rows_of(c), :] = (slot[rows_of(c), :].astype(jnp.float32) * precond_ref[...]).astype(jnp.bfloat16)

    def send_own(c):
        pl.when(z < n_row - 1)(lambda: hop(0, z, c).start())
        pl.when(z > 0)(lambda: hop(1, z, c).start())

    def product(b, c):
        weighted = blocks[b, rows_of(c), :]
        for r in PART_ORDER(n_dim):
            to = lax.rem(d + r, n_dim)
            mine = train[pl.ds(pl.multiple_of(to * share, share), share), :]
            part = lax.dot_general(mine, weighted, NT, preferred_element_type=jnp.float32)
            parts[b, c, to] = part.astype(jnp.bfloat16)
            if r:
                send_part(b, c, r).start()

    def add_up(b, c):
        for r in range(1, n_dim):
            send_part(b, c, r).wait_recv()
        total = parts[b, c, d].astype(jnp.float32)
        for r in range(1, n_dim):
            total = total + landed[b, c, lax.rem(d + r, n_dim)].astype(jnp.float32)
        raw_ref[b, c] = total

    def each_block(h, run):
        if h == 0:
            run(z)
        elif h < n_row:
            pl.when(z - h >= 0)(lambda: run(z - h))
            pl.when(z + h < n_row)(lambda: run(z + h))

    load_precond.wait()
    load_slot.wait()
    for c in range(AHEAD):
        weigh(c)
    pl.semaphore_wait(barrier, n_row - 1 + n_dim - 1)
    for c in range(AHEAD):
        send_own(c)
    for c in range(AHEAD, steps):
        weigh(c)

    q_out[...] = jnp.broadcast_to(row_sums(slot[...], precond_ref[...]), q_out.shape)

    def norm_copy(r, which):
        to = lax.rem(d + r, n_dim)
        src, dst = (g_out.at[to], g_in.at[d]) if which == 0 else (q_out, q_in.at[d])
        return pltpu.make_async_remote_copy(
            src_ref=src, dst_ref=dst, send_sem=norm_send.at[which, r], recv_sem=norm_recv.at[which, r],
            device_id={"dim": to}, device_id_type=MESH,
        )

    def q_copy(r):
        return pltpu.make_async_remote_copy(
            src_ref=q_sum, dst_ref=q_all.at[z], send_sem=q_send.at[r], recv_sem=q_recv.at[r],
            device_id={"row": lax.rem(z + r, n_row)}, device_id_type=MESH,
        )

    for r in range(1, n_dim):
        norm_copy(r, 1).start()
    load_train.wait()

    def train_norms(t):
        at = pl.ds(pl.multiple_of(t * share, share), share)
        g_out[t] = jnp.broadcast_to(row_sums(train[at, :], precond_ref[...]), g_out.shape[1:])

    for h in range(1, n_row):

        def step(c, carry, h=h):
            def arrive_left():
                hop(0, z - h, c).wait_recv()
                pl.when(z < n_row - 1)(lambda: hop(0, z - h, c).start())

            def arrive_right():
                hop(1, z + h, c).wait_recv()
                pl.when(z > 0)(lambda: hop(1, z + h, c).start())

            if h == 1:
                product(z, c)
            pl.when(z - h >= 0)(arrive_left)
            pl.when(z + h < n_row)(arrive_right)
            if h == 1:
                pl.when(c + AHEAD < steps)(lambda: send_own(c + AHEAD))
            each_block(h, lambda b: product(b, c))
            if h > 1:
                pl.when(c == 0)(lambda: each_block(h - 1, lambda b: add_up(b, steps - 1)))
            pl.when(c > 0)(lambda: each_block(h, lambda b: add_up(b, c - 1)))
            if h == 1:
                pl.when(c < n_dim)(lambda: train_norms(c))
            return carry

        lax.fori_loop(0, steps, step, 0)
        if h == 1:
            for t in range(steps, n_dim):
                train_norms(t)
            for r in range(1, n_dim):
                norm_copy(r, 0).start()
            for r in range(1, n_dim):
                norm_copy(r, 1).wait_recv()
            total = q_out[...]
            for r in range(1, n_dim):
                total = total + q_in[lax.rem(d + r, n_dim)]
            q_sum[...] = total
            q_ref[z] = lax.rsqrt(total / K + 1e-06)
            for r in range(1, n_row):
                q_copy(r).start()
            for c in range(steps):
                add_up(z, c)
            for r in range(1, n_dim):
                norm_copy(r, 0).wait_recv()
            total = g_out[d]
            for r in range(1, n_dim):
                total = total + g_in[lax.rem(d + r, n_dim)]
            g = lax.rsqrt(K * (total[0:1, :] / K + 1e-06))
            column[...] = jnp.broadcast_to(g, (128, share)).T
        if h == 2:
            for r in range(1, n_row):
                q_copy(r).wait_recv()
            for r in range(1, n_row):
                other = lax.rem(z + r, n_row)
                q_ref[other] = lax.rsqrt(q_all[other] / K + 1e-06)
    each_block(n_row - 1, lambda b: add_up(b, steps - 1))
    load_owner.wait()
    load_order.wait()
    for s in range(NB):
        root = owner_ref[order_ref[s]]
        q = q_ref[root]
        for c in range(steps):
            at = slice(c * CHUNK, (c + 1) * CHUNK)
            out_ref[s, :, at] = raw_ref[root, c] * column[...] * q[0:1, at]

    def sent(c, carry):
        for b in range(n_row):
            pl.when((z < n_row - 1) & (b <= z))(lambda b=b: hop(0, b, c).wait_send())
            pl.when((z > 0) & (b >= z))(lambda b=b: hop(1, b, c).wait_send())
            for r in range(1, n_dim):
                send_part(b, c, r).wait_send()
        return carry

    lax.fori_loop(0, steps, sent, 0)
    for r in range(1, n_dim):
        norm_copy(r, 0).wait_send()
        norm_copy(r, 1).wait_send()
    for r in range(1, n_row):
        q_copy(r).wait_send()


def PART_ORDER(n_dim):
    middle = n_dim // 2
    return [middle] + [r for r in range(1, n_dim) if r != middle] + [0]


def scores(n_row, n_dim, owner, order, train_grads, precond, slot):
    rows, width = train_grads.shape
    queries = slot.shape[0]
    share = rows // n_dim
    steps = queries // CHUNK
    f32, bf16 = jnp.float32, jnp.bfloat16
    vmem = pl.BlockSpec(memory_space=pltpu.VMEM)
    hbm = pl.BlockSpec(memory_space=pltpu.HBM)
    dma = pltpu.SemaphoreType.DMA
    return pl.pallas_call(
        functools.partial(score_kernel, n_row, n_dim),
        out_shape=jax.ShapeDtypeStruct((NB, share, queries), f32),
        in_specs=[hbm, hbm, hbm, hbm, hbm],
        out_specs=vmem,
        scratch_shapes=[
            pltpu.SMEM((NB,), jnp.int32),
            pltpu.SMEM((NB,), jnp.int32),
            pltpu.VMEM((n_row, steps, share, CHUNK), f32),
            pltpu.VMEM((share, 128), f32),
            pltpu.VMEM((n_row, 8, queries), f32),
            pltpu.VMEM((rows, width), bf16),
            pltpu.VMEM((1, width), f32),
            pltpu.VMEM((queries, width), bf16),
            pltpu.VMEM((n_row, queries, width), bf16),
            pltpu.VMEM((n_row, steps, n_dim, share, CHUNK), bf16),
            pltpu.VMEM((n_row, steps, n_dim, share, CHUNK), bf16),
            pltpu.VMEM((n_dim, 8, share), f32),
            pltpu.VMEM((n_dim, 8, share), f32),
            pltpu.VMEM((8, queries), f32),
            pltpu.VMEM((n_dim, 8, queries), f32),
            pltpu.VMEM((8, queries), f32),
            pltpu.VMEM((n_row, 8, queries), f32),
            dma((5,)),
            dma((2, n_row, steps)),
            dma((n_row, steps)),
            dma((n_row, n_dim, steps)),
            dma((n_row, n_dim, steps)),
            dma((2, n_dim)),
            dma((2, n_dim)),
            dma((n_row,)),
            dma((n_row,)),
        ],
        compiler_params=pltpu.CompilerParams(
            collective_id=0, has_side_effects=True, vmem_limit_bytes=VMEM_MIB * 1024 * 1024
        ),
        name="scores",
    )(owner, order, train_grads, precond.reshape(1, width), slot)


def every_slot(train_grads, precond, query_store, owner, order):
    return scores(lax.axis_size("row"), lax.axis_size("dim"), owner, order, train_grads, precond, query_store[0])


def weighted_norm(values, precond):
    wide = values.astype(jnp.float32)
    return jnp.sum(wide * wide * precond[None, :], axis=1) / K


def some_slots(train_grads, precond, query_store, owner, order):
    share = train_grads.shape[0] // lax.axis_size("dim")
    slot = query_store[0]
    roots = owner[order]
    mine = (roots == lax.axis_index("row"))[:, None, None]
    blocks = lax.psum(jnp.where(mine, slot[None], 0).astype(jnp.bfloat16), "row")
    gsq = lax.psum_scatter(weighted_norm(train_grads, precond), "dim", tiled=True)
    results = []
    for step in range(NB):
        block = blocks[step]
        qsq = lax.psum(weighted_norm(block, precond), "dim")
        weighted = (block.astype(jnp.float32) * precond[None, :]).astype(jnp.bfloat16)
        part = lax.dot_general(train_grads, weighted, NT, preferred_element_type=jnp.float32)
        summed = lax.psum_scatter(part.astype(jnp.bfloat16), "dim", scatter_dimension=0, tiled=True)
        scale = jnp.sqrt(K * (gsq[:, None] + 1e-06) * (qsq[None, :] + 1e-06))
        results.append(summed.astype(jnp.float32) / scale)
    return jnp.stack(results)


def solution(mesh):
    return jax.shard_map(
        every_slot if mesh.shape["row"] == NB else some_slots,
        mesh=mesh,
        in_specs=(
            P(("parts", "row"), "dim"),
            P("dim"),
            P(("parts", "row"), None, "dim"),
            P("parts"),
            P("parts"),
        ),
        out_specs=P(None, ("parts", "row", "dim"), None),
        check_vma=False,
    )
```
